512 devices in a mesh: row: 64 (over z, x_lo, core), col: 8 (over x_hi, y).
Axes of the slice: x: 4 (x_hi: 2, x_lo: 2; x = x_hi * 2 + x_lo), y: 4, z: 16, core: 2. Of those that a mesh axis runs over, the one named last changes fastest.
Arguments:
- tokens: bfloat16 [1024, 4096], P('row', 'col'), may hold values from -6 to 6
- probe_draw: int32 [1024, 4096], P(None, 'col'), may hold values from 0 to 1
- w_in: bfloat16 [4096, 16384], P('col', 'row'), may hold values from -0.09375 to 0.09375
- w_out: bfloat16 [16384, 4096], P('row', 'col'), may hold values from -0.09375 to 0.09375
Outputs:
- grad_in: float32 [4096, 16384], P('col', 'row')
- grad_out: float32 [16384, 4096], P('row', 'col')
The draws below stay inside these ranges and needn't reach their ends.
All inputs are finite; a program needn't handle non-finite values.
Results may differ from the reference program's by a relative error of at most 0.013.
Values may be sent and summed in bfloat16 or wider, within the bound.
No kernel may reach another device: no remote copies, remote signals or barrier semaphores. Data moves between devices by JAX's collectives and lax.ppermute only.
A program may use at most 64 MiB of HBM per device.

```python
import jax
import jax.numpy as jnp
from jax import lax

D = 4096
FF = 16384
TOKENS = 1024


def touch_ends(entries, key, least, largest):
    longest = entries.shape.index(max(entries.shape))
    spots = []
    for shift in (0, 1):
        where = [jax.random.randint(jax.random.fold_in(key, axis), (), 0, length) for axis, length in enumerate(entries.shape)]
        where[longest] = (where[longest] + shift) % entries.shape[longest]
        spots.append(tuple(where))
    return entries.at[spots[0]].set(least).at[spots[1]].set(largest)


def block_levels(rng, extent, cuts, low, top_value):
    loudness, own = 1.0, jax.random.fold_in(rng, 6)
    for axis_at, parts in cuts:
        steps = jnp.exp(jax.random.uniform(jax.random.fold_in(own, axis_at), (parts,), jnp.float32, low / len(cuts), top_value / len(cuts)))
        loudness = loudness * jnp.repeat(steps, extent[axis_at] // parts).reshape([-1 if axis == axis_at else 1 for axis in range(len(extent))])
    return loudness


def centred(stream_key, shape, width, limit, cuts=(), held_as=jnp.bfloat16):
    array = width * jax.random.normal(stream_key, shape, jnp.float32)
    if cuts:
        array = array * block_levels(stream_key, shape, cuts, -0.22, 0.18)
    return jnp.clip(array, -limit, limit).astype(held_as)


def setup_inputs(seed: int = 0) -> dict:
    key_of = jax.random.split(jax.random.key(seed), 5)
    tokens = centred(key_of[0], (TOKENS, D), 1.0, 6.0, ((0, 64), (1, 8)))
    probe_draw = touch_ends(jax.random.randint(key_of[1], (TOKENS, D), 0, 2), jax.random.fold_in(key_of[1], 1), 0, 1).astype(jnp.int32)
    w_in = centred(key_of[2], (D, FF), D ** -0.5, 0.09375, ((0, 8), (1, 64)))
    w_out = centred(key_of[3], (FF, D), D ** -0.5, 0.09375, ((0, 64), (1, 8)))
    return {"tokens": tokens, "probe_draw": probe_draw, "w_in": w_in, "w_out": w_out}


def local_terms(hidden, signal):
    cdf_part = 0.5 * (1.0 + lax.erf(hidden * 0.7071067811865476))
    pdf_part = jnp.exp(-0.5 * hidden * hidden) * 0.3989422804014327
    slope_full = cdf_part + hidden * pdf_part
    slopes = slope_full.astype(jnp.bfloat16)
    bending = (signal * pdf_part * (2.0 - hidden * hidden)).astype(jnp.bfloat16)
    gated = (signal * slope_full).astype(jnp.bfloat16)
    return (slopes, bending, gated)

def reference(tokens, probe_draw, w_in, w_out):
    sign_values = (2 * probe_draw - 1).astype(jnp.bfloat16)
    hidden = jnp.dot(tokens, w_in, preferred_element_type=jnp.float32)
    signal = jnp.dot(sign_values, w_out.T, preferred_element_type=jnp.float32)
    slopes, bending, gated = local_terms(hidden, signal)
    jac_rows = jnp.dot(gated, w_in.T, preferred_element_type=jnp.float32).astype(jnp.bfloat16)
    back_proj = jnp.dot(jac_rows, w_in, preferred_element_type=jnp.float32)
    curv_term = (back_proj * bending).astype(jnp.bfloat16)
    slope_term = (back_proj * slopes).astype(jnp.bfloat16)
    factor = 1.0 / jnp.sqrt(jnp.float32(TOKENS))
    grad_in = factor * (jnp.dot(tokens.T, curv_term, preferred_element_type=jnp.float32) + jnp.dot(jac_rows.T, gated, preferred_element_type=jnp.float32))
    grad_out = factor * jnp.dot(slope_term.T, sign_values, preferred_element_type=jnp.float32)
    return (grad_in, grad_out)
```

```python
import jax
import jax.numpy as jnp
from jax import lax
from jax.sharding import Mesh, PartitionSpec as P

Z, NEAR, COL = ("z",), ("xl", "core"), ("xh", "y")
BF, F32 = jnp.bfloat16, jnp.float32


def local_terms(hidden, signal):
    cdf_part = 0.5 * (1.0 + lax.erf(hidden * 0.7071067811865476))
    pdf_part = jnp.exp(-0.5 * hidden * hidden) * 0.3989422804014327
    slope_full = cdf_part + hidden * pdf_part
    slopes = slope_full.astype(BF)
    bending = (signal * pdf_part * (2.0 - hidden * hidden)).astype(BF)
    gated = (signal * slope_full).astype(BF)
    return (slopes, bending, gated)


def contract_rows(left, right):
    return lax.dot_general(
        left, right, (((0,), (0,)), ((), ())), preferred_element_type=F32
    )


def contract_cols(left, right):
    return lax.dot_general(
        left, right, (((1,), (1,)), ((), ())), preferred_element_type=F32
    )


def exchange(blocks, axes):
    return lax.all_to_all(blocks, axes, 0, 0, tiled=True)


def gather(block, axes, count):
    rows, cols = block.shape
    return exchange(
        jnp.broadcast_to(block[None], (count, rows, cols)), axes
    ).reshape(count * rows, cols)


def scatter_sum(array, axes, count):
    rows, cols = array.shape
    blocks = array.astype(BF).reshape(count, rows // count, cols)
    return exchange(blocks, axes).astype(F32).sum(axis=0)


def on_device(tokens, probe_draw, w_in, w_out):
    total_rows = probe_draw.shape[0]
    own_rows, feats = tokens.shape
    nz, nn, nc = (lax.axis_size(a) for a in (Z, NEAR, COL))
    hid = w_in.shape[1]
    sign_values = (2 * probe_draw - 1).astype(BF)
    sign_values = (
        sign_values.reshape(nz, nn, own_rows, feats)
        .transpose(1, 0, 2, 3)
        .reshape(total_rows, feats)
    )
    signal_part = contract_cols(sign_values, w_out)
    token_full = gather(gather(tokens, Z, nz), NEAR, nn)
    hidden_part = jnp.dot(token_full, w_in, preferred_element_type=F32)
    both = scatter_sum(
        jnp.concatenate([hidden_part, signal_part], axis=1), COL, nc
    )
    slopes, bending, gated_own = local_terms(both[:, :hid], both[:, hid:])
    gated = gather(gated_own, COL, nc)
    jac_part = contract_cols(gated, w_in)
    jac_own = scatter_sum(scatter_sum(jac_part, NEAR, nn), Z, nz).astype(BF)
    jac_rows = gather(gather(jac_own, Z, nz), NEAR, nn)
    back_part = jnp.dot(jac_rows, w_in, preferred_element_type=F32)
    back_proj = scatter_sum(back_part, COL, nc)
    curv_own = (back_proj * bending).astype(BF)
    slope_own = (back_proj * slopes).astype(BF)
    terms = gather(jnp.concatenate([curv_own, slope_own], axis=1), COL, nc)
    curv_term, slope_term = terms[:, :hid], terms[:, hid:]
    factor = 1.0 / jnp.sqrt(jnp.float32(total_rows))
    grad_in = factor * (
        contract_rows(token_full, curv_term) + contract_rows(jac_rows, gated)
    )
    grad_out = factor * contract_rows(slope_term, sign_values)
    return (grad_in, grad_out)


def solution(mesh):
    fine = Mesh(
        mesh.devices.reshape(16, 2, 2, 2, 4), ("z", "xl", "core", "xh", "y")
    )
    row, col = Z + NEAR, COL
    return jax.shard_map(
        on_device,
        mesh=fine,
        in_specs=(P(row, col), P(None, col), P(col, row), P(row, col)),
        out_specs=(P(col, row), P(row, col)),
        check_vma=False,
    )
```

```python
import jax
import jax.numpy as jnp
from jax import lax
from jax.sharding import Mesh, PartitionSpec as P

LINE, COL = ("z", "xl"), ("xh", "y")
BF, F32 = jnp.bfloat16, jnp.float32


def local_terms(hidden, signal):
    cdf_part = 0.5 * (1.0 + lax.erf(hidden * 0.7071067811865476))
    pdf_part = jnp.exp(-0.5 * hidden * hidden) * 0.3989422804014327
    slope_full = cdf_part + hidden * pdf_part
    slopes = slope_full.astype(BF)
    bending = (signal * pdf_part * (2.0 - hidden * hidden)).astype(BF)
    gated = (signal * slope_full).astype(BF)
    return (slopes, bending, gated)


def contract_rows(left, right):
    return lax.dot_general(
        left, right, (((0,), (0,)), ((), ())), preferred_element_type=F32
    )


def contract_cols(left, right):
    return lax.dot_general(
        left, right, (((1,), (1,)), ((), ())), preferred_element_type=F32
    )


def exchange(blocks, axes):
    return lax.all_to_all(blocks, axes, 0, 0, tiled=True)


def gather(block, axes, count):
    rows, cols = block.shape
    return exchange(
        jnp.broadcast_to(block[None], (count, rows, cols)), axes
    ).reshape(count * rows, cols)


def scatter_sum(array, axes, count):
    rows, cols = array.shape
    blocks = array.astype(BF).reshape(count, rows // count, cols)
    return exchange(blocks, axes).astype(F32).sum(axis=0)


def other_core(array):
    return lax.ppermute(array, "core", [(0, 1), (1, 0)])


def on_device(tokens, probe_draw, w_in, w_out):
    total_rows = probe_draw.shape[0]
    own_rows, feats = tokens.shape
    nl, nc = lax.axis_size(LINE), lax.axis_size(COL)
    hid = w_in.shape[1]
    w_in_pair = jnp.concatenate([w_in, other_core(w_in)], axis=1)
    w_out_pair = jnp.concatenate([w_out, other_core(w_out)], axis=0)
    draw = lax.dynamic_index_in_dim(
        probe_draw.reshape(nl, 2, own_rows, feats),
        lax.axis_index("core"),
        axis=1,
        keepdims=False,
    ).reshape(nl * own_rows, feats)
    sign_values = (2 * draw - 1).astype(BF)
    signal_part = contract_cols(sign_values, w_out_pair)
    token_part = gather(tokens, LINE, nl)
    hidden_part = jnp.dot(token_part, w_in_pair, preferred_element_type=F32)
    both = scatter_sum(
        jnp.concatenate([hidden_part, signal_part], axis=1), COL, nc
    )
    slopes, bending, gated_own = local_terms(
        both[:, : 2 * hid], both[:, 2 * hid :]
    )
    gated = gather(gated_own, COL, nc)
    jac_own = scatter_sum(contract_cols(gated, w_in_pair), LINE, nl).astype(BF)
    jac_rows = gather(jac_own, LINE, nl)
    back_part = jnp.dot(jac_rows, w_in_pair, preferred_element_type=F32)
    back_proj = scatter_sum(back_part, COL, nc)
    curv_own = (back_proj * bending).astype(BF)
    slope_own = (back_proj * slopes).astype(BF)
    terms = gather(jnp.concatenate([curv_own, slope_own], axis=1), COL, nc)
    curv_term, slope_term = terms[:, : 2 * hid], terms[:, 2 * hid :]
    factor = 1.0 / jnp.sqrt(jnp.float32(total_rows))

    def grads(part):
        return (
            contract_rows(token_part, curv_term[:, part])
            + contract_rows(jac_rows, gated[:, part]),
            contract_rows(slope_term[:, part], sign_values),
        )

    in_far, out_far = grads(slice(hid, 2 * hid))
    in_near, out_near = grads(slice(0, hid))
    return (
        factor * (in_near + other_core(in_far)),
        factor * (out_near + other_core(out_far)),
    )


def solution(mesh):
    fine = Mesh(
        mesh.devices.reshape(16, 2, 2, 2, 4), ("z", "xl", "core", "xh", "y")
    )
    row, col = LINE + ("core",), COL
    return jax.shard_map(
        on_device,
        mesh=fine,
        in_specs=(P(row, col), P(None, col), P(col, row), P(row, col)),
        out_specs=(P(col, row), P(row, col)),
        check_vma=False,
    )
```

```python
import jax
import jax.numpy as jnp
from jax import lax
from jax.sharding import Mesh, PartitionSpec as P

NEAR, COL = ("core", "xl"), ("xh", "y")
BF, F32 = jnp.bfloat16, jnp.float32


def local_terms(hidden, signal):
    cdf_part = 0.5 * (1.0 + lax.erf(hidden * 0.7071067811865476))
    pdf_part = jnp.exp(-0.5 * hidden * hidden) * 0.3989422804014327
    slope_full = cdf_part + hidden * pdf_part
    slopes = slope_full.astype(BF)
    bending = (signal * pdf_part * (2.0 - hidden * hidden)).astype(BF)
    gated = (signal * slope_full).astype(BF)
    return (slopes, bending, gated)


def contract_rows(left, right):
    return lax.dot_general(
        left, right, (((0,), (0,)), ((), ())), preferred_element_type=F32
    )


def contract_cols(left, right):
    return lax.dot_general(
        left, right, (((1,), (1,)), ((), ())), preferred_element_type=F32
    )


def exchange(blocks, axes):
    return lax.all_to_all(blocks, axes, 0, 0, tiled=True)


def gather(block, axes, count):
    rows, cols = block.shape
    return exchange(
        jnp.broadcast_to(block[None], (count, rows, cols)), axes
    ).reshape(count * rows, cols)


def scatter_sum(array, axes, count):
    rows, cols = array.shape
    blocks = array.astype(BF).reshape(count, rows // count, cols)
    return exchange(blocks, axes).astype(F32).sum(axis=0)


def pair_up(array, name, axis):
    far = lax.ppermute(array, name, [(0, 1), (1, 0)])
    return jnp.where(
        lax.axis_index(name) == 0,
        jnp.concatenate([array, far], axis=axis),
        jnp.concatenate([far, array], axis=axis),
    )


def on_device(tokens, probe_draw, w_in, w_out):
    total_rows = probe_draw.shape[0]
    own_rows, feats = tokens.shape
    nz, nn, nc = (lax.axis_size(a) for a in ("z", NEAR, COL))
    hid = w_in.shape[1]
    wide = nn * hid
    near = lax.axis_index(NEAR)
    w_in_all = pair_up(pair_up(w_in, "xl", 1), "core", 1)
    w_out_all = pair_up(pair_up(w_out, "xl", 0), "core", 0)
    draw = probe_draw.reshape(nz, nn, own_rows, feats)
    sign_all = (
        (2 * probe_draw - 1)
        .astype(BF)
        .reshape(nz, 2, 2, own_rows, feats)
        .transpose(2, 1, 0, 3, 4)
        .reshape(total_rows, feats)
    )
    mine = lax.axis_index(("xl", "core"))
    own_draw = lax.dynamic_index_in_dim(draw, mine, axis=1, keepdims=False)
    own_sign = (2 * own_draw - 1).astype(BF).reshape(nz * own_rows, feats)
    signal_part = contract_cols(own_sign, w_out_all)
    own_tokens = gather(tokens, "z", nz)
    all_tokens = lax.all_gather(own_tokens, NEAR, axis=0, tiled=True)
    hidden_part = jnp.dot(own_tokens, w_in_all, preferred_element_type=F32)
    both = scatter_sum(
        jnp.concatenate([hidden_part, signal_part], axis=1), COL, nc
    )
    slopes, bending, gated_own = local_terms(both[:, :wide], both[:, wide:])
    gated = gather(gated_own, COL, nc)
    gated_all = lax.all_gather(gated, NEAR, axis=0, tiled=True)
    gated_hid = lax.dynamic_slice_in_dim(gated_all, near * hid, hid, axis=1)
    jac_own = scatter_sum(contract_cols(gated, w_in_all), "z", nz).astype(BF)
    jac_rows = gather(jac_own, "z", nz)
    jac_all = lax.all_gather(jac_rows, NEAR, axis=0, tiled=True)
    back_part = jnp.dot(jac_rows, w_in_all, preferred_element_type=F32)
    back_proj = scatter_sum(back_part, COL, nc)
    rows = back_proj.shape[0]
    curv_own = (back_proj * bending).astype(BF).reshape(rows, nn, hid)
    slope_own = (back_proj * slopes).astype(BF).reshape(rows, nn, hid)
    terms = jnp.concatenate([curv_own, slope_own], axis=2).transpose(1, 0, 2)
    terms = jnp.broadcast_to(terms[:, None], (nn, nc, rows, 2 * hid))
    terms = exchange(
        terms.reshape(nn * nc, rows, 2 * hid), NEAR + COL
    ).reshape(total_rows, 2 * hid)
    curv_term, slope_term = terms[:, :hid], terms[:, hid:]
    factor = 1.0 / jnp.sqrt(jnp.float32(total_rows))
    grad_in = factor * (
        contract_rows(all_tokens, curv_term) + contract_rows(jac_all, gated_hid)
    )
    grad_out = factor * contract_rows(slope_term, sign_all)
    return (grad_in, grad_out)


def solution(mesh):
    fine = Mesh(
        mesh.devices.reshape(16, 2, 2, 2, 4), ("z", "xl", "core", "xh", "y")
    )
    row, col = ("z", "xl", "core"), COL
    return jax.shard_map(
        on_device,
        mesh=fine,
        in_specs=(P(row, col), P(None, col), P(col, row), P(row, col)),
        out_specs=(P(col, row), P(row, col)),
        check_vma=False,
    )
```

```python
import jax
import jax.numpy as jnp
from jax import lax
from jax.sharding import Mesh, PartitionSpec as P

NEAR, COL = ("core", "xl"), ("xh", "y")
BF, F32 = jnp.bfloat16, jnp.float32


def local_terms(hidden, signal):
    cdf_part = 0.5 * (1.0 + lax.erf(hidden * 0.7071067811865476))
    pdf_part = jnp.exp(-0.5 * hidden * hidden) * 0.3989422804014327
    slope_full = cdf_part + hidden * pdf_part
    slopes = slope_full.astype(BF)
    bending = (signal * pdf_part * (2.0 - hidden * hidden)).astype(BF)
    gated = (signal * slope_full).astype(BF)
    return (slopes, bending, gated)


def contract_rows(left, right):
    return lax.dot_general(
        left, right, (((0,), (0,)), ((), ())), preferred_element_type=F32
    )


def contract_cols(left, right):
    return lax.dot_general(
        left, right, (((1,), (1,)), ((), ())), preferred_element_type=F32
    )


def exchange(blocks, axes):
    return lax.all_to_all(blocks, axes, 0, 0, tiled=True)


def gather(block, axes, count):
    rows, cols = block.shape
    return exchange(
        jnp.broadcast_to(block[None], (count, rows, cols)), axes
    ).reshape(count * rows, cols)


def scatter_sum(array, axes, count):
    rows, cols = array.shape
    blocks = array.astype(BF).reshape(count, rows // count, cols)
    return exchange(blocks, axes).astype(F32).sum(axis=0)


def pair_up(array, name, axis):
    far = lax.ppermute(array, name, [(0, 1), (1, 0)])
    return jnp.where(
        lax.axis_index(name) == 0,
        jnp.concatenate([array, far], axis=axis),
        jnp.concatenate([far, array], axis=axis),
    )


def hand_over(array, name, axis):
    half = array.shape[-1] // 2
    left, right = array[..., :half], array[..., half:]
    first = lax.axis_index(name) == 0
    kept = jnp.where(first, left, right)
    far = lax.ppermute(
        jnp.where(first, right, left), name, [(0, 1), (1, 0)]
    )
    return jnp.where(
        first,
        jnp.concatenate([kept, far], axis=axis),
        jnp.concatenate([far, kept], axis=axis),
    )


def on_device(tokens, probe_draw, w_in, w_out):
    total_rows = probe_draw.shape[0]
    own_rows, feats = tokens.shape
    nz, nn, nc = (lax.axis_size(a) for a in ("z", NEAR, COL))
    hid = w_in.shape[1]
    wide = nn * hid
    w_in_all = pair_up(pair_up(w_in, "xl", 1), "core", 1)
    w_out_all = pair_up(pair_up(w_out, "xl", 0), "core", 0)
    draw = probe_draw.reshape(nz, nn, own_rows, feats)
    sign_all = (
        (2 * probe_draw - 1)
        .astype(BF)
        .reshape(nz, 2, 2, own_rows, feats)
        .transpose(2, 1, 0, 3, 4)
        .reshape(total_rows, feats)
    )
    mine = lax.axis_index(("xl", "core"))
    own_draw = lax.dynamic_index_in_dim(draw, mine, axis=1, keepdims=False)
    own_sign = (2 * own_draw - 1).astype(BF).reshape(nz * own_rows, feats)
    signal_part = contract_cols(own_sign, w_out_all)
    own_tokens = gather(tokens, "z", nz)
    all_tokens = pair_up(pair_up(own_tokens, "xl", 0), "core", 0)
    hidden_part = jnp.dot(own_tokens, w_in_all, preferred_element_type=F32)
    both = scatter_sum(
        jnp.concatenate([hidden_part, signal_part], axis=1), COL, nc
    )
    slopes, bending, gated_own = local_terms(both[:, :wide], both[:, wide:])
    gated = gather(gated_own, COL, nc)
    gated_hid = hand_over(hand_over(gated[None], "core", 0), "xl", 1)
    gated_hid = gated_hid.reshape(total_rows, hid)
    jac_own = scatter_sum(contract_cols(gated, w_in_all), "z", nz).astype(BF)
    jac_rows = gather(jac_own, "z", nz)
    jac_all = pair_up(pair_up(jac_rows, "xl", 0), "core", 0)
    back_part = jnp.dot(jac_rows, w_in_all, preferred_element_type=F32)
    back_proj = scatter_sum(back_part, COL, nc)
    rows = back_proj.shape[0]
    curv_own = (back_proj * bending).astype(BF).reshape(rows, nn, hid)
    slope_own = (back_proj * slopes).astype(BF).reshape(rows, nn, hid)
    terms = jnp.concatenate([curv_own, slope_own], axis=2).transpose(1, 0, 2)
    terms = jnp.broadcast_to(terms[:, None], (nn, nc, rows, 2 * hid))
    terms = exchange(
        terms.reshape(nn * nc, rows, 2 * hid), NEAR + COL
    ).reshape(total_rows, 2 * hid)
    curv_term, slope_term = terms[:, :hid], terms[:, hid:]
    factor = 1.0 / jnp.sqrt(jnp.float32(total_rows))
    grad_in = factor * (
        contract_rows(all_tokens, curv_term) + contract_rows(jac_all, gated_hid)
    )
    grad_out = factor * contract_rows(slope_term, sign_all)
    return (grad_in, grad_out)


def solution(mesh):
    fine = Mesh(
        mesh.devices.reshape(16, 2, 2, 2, 4), ("z", "xl", "core", "xh", "y")
    )
    row, col = ("z", "xl", "core"), COL
    return jax.shard_map(
        on_device,
        mesh=fine,
        in_specs=(P(row, col), P(None, col), P(col, row), P(row, col)),
        out_specs=(P(col, row), P(row, col)),
        check_vma=False,
    )
```

```python
import jax
import jax.numpy as jnp
from jax import lax
from jax.sharding import Mesh, PartitionSpec as P

NEAR, COL = ("core", "xl"), ("xh", "y")
BF, F32 = jnp.bfloat16, jnp.float32


def local_terms(hidden, signal):
    cdf_part = 0.5 * (1.0 + lax.erf(hidden * 0.7071067811865476))
    pdf_part = jnp.exp(-0.5 * hidden * hidden) * 0.3989422804014327
    slope_full = cdf_part + hidden * pdf_part
    slopes = slope_full.astype(BF)
    bending = (signal * pdf_part * (2.0 - hidden * hidden)).astype(BF)
    gated = (signal * slope_full).astype(BF)
    return (slopes, bending, gated)


def contract_rows(left, right):
    return lax.dot_general(
        left, right, (((0,), (0,)), ((), ())), preferred_element_type=F32
    )


def contract_cols(left, right):
    return lax.dot_general(
        left, right, (((1,), (1,)), ((), ())), preferred_element_type=F32
    )


def exchange(blocks, axes):
    return lax.all_to_all(blocks, axes, 0, 0, tiled=True)


def gather(block, axes, count):
    rows, cols = block.shape
    return exchange(
        jnp.broadcast_to(block[None], (count, rows, cols)), axes
    ).reshape(count * rows, cols)


def scatter_sum(array, axes, count):
    rows, cols = array.shape
    blocks = array.astype(BF).reshape(count, rows // count, cols)
    return exchange(blocks, axes).astype(F32).sum(axis=0)


def pair_up(array, name, axis):
    far = lax.ppermute(array, name, [(0, 1), (1, 0)])
    return jnp.where(
        lax.axis_index(name) == 0,
        jnp.concatenate([array, far], axis=axis),
        jnp.concatenate([far, array], axis=axis),
    )


def hand_over(array, name, axis):
    half = array.shape[-1] // 2
    left, right = array[..., :half], array[..., half:]
    first = lax.axis_index(name) == 0
    kept = jnp.where(first, left, right)
    far = lax.ppermute(
        jnp.where(first, right, left), name, [(0, 1), (1, 0)]
    )
    return jnp.where(
        first,
        jnp.concatenate([kept, far], axis=axis),
        jnp.concatenate([far, kept], axis=axis),
    )


def beside(chain, operand):
    return lax.optimization_barrier((chain, operand))


def on_device(tokens, probe_draw, w_in, w_out):
    total_rows = probe_draw.shape[0]
    own_rows, feats = tokens.shape
    nz, nn, nc = (lax.axis_size(a) for a in ("z", NEAR, COL))
    hid = w_in.shape[1]
    wide = nn * hid
    w_in_all = pair_up(pair_up(w_in, "xl", 1), "core", 1)
    w_out_all = pair_up(pair_up(w_out, "xl", 0), "core", 0)
    draw = probe_draw.reshape(nz, nn, own_rows, feats)
    sign_all = (
        (2 * probe_draw - 1)
        .astype(BF)
        .reshape(nz, 2, 2, own_rows, feats)
        .transpose(2, 1, 0, 3, 4)
        .reshape(total_rows, feats)
    )
    mine = lax.axis_index(("xl", "core"))
    own_draw = lax.dynamic_index_in_dim(draw, mine, axis=1, keepdims=False)
    own_sign = (2 * own_draw - 1).astype(BF).reshape(nz * own_rows, feats)
    signal_part = contract_cols(own_sign, w_out_all)
    own_tokens = gather(tokens, "z", nz)
    token_pair = pair_up(own_tokens, "xl", 0)
    hidden_part = jnp.dot(own_tokens, w_in_all, preferred_element_type=F32)
    both = scatter_sum(
        jnp.concatenate([hidden_part, signal_part], axis=1), COL, nc
    )
    both, token_pair = beside(both, token_pair)
    slopes, bending, gated_own = local_terms(both[:, :wide], both[:, wide:])
    gated = gather(gated_own, COL, nc)
    all_tokens = pair_up(token_pair, "core", 0)
    gated, all_tokens = beside(gated, all_tokens)
    gated_pair = hand_over(gated[None], "core", 0)
    jac_own = scatter_sum(contract_cols(gated, w_in_all), "z", nz).astype(BF)
    jac_own, gated_pair = beside(jac_own, gated_pair)
    gated_hid = hand_over(gated_pair, "xl", 1).reshape(total_rows, hid)
    jac_rows = gather(jac_own, "z", nz)
    jac_rows, gated_hid = beside(jac_rows, gated_hid)
    jac_pair = pair_up(jac_rows, "xl", 0)
    back_part = jnp.dot(jac_rows, w_in_all, preferred_element_type=F32)
    back_proj = scatter_sum(back_part, COL, nc)
    back_proj, jac_pair = beside(back_proj, jac_pair)
    jac_all = pair_up(jac_pair, "core", 0)
    rows = back_proj.shape[0]
    curv_own = (back_proj * bending).astype(BF).reshape(rows, nn, hid)
    slope_own = (back_proj * slopes).astype(BF).reshape(rows, nn, hid)
    terms = jnp.concatenate([curv_own, slope_own], axis=2).transpose(1, 0, 2)
    terms = jnp.broadcast_to(terms[:, None], (nn, nc, rows, 2 * hid))
    terms = exchange(
        terms.reshape(nn * nc, rows, 2 * hid), NEAR + COL
    ).reshape(total_rows, 2 * hid)
    curv_term, slope_term = terms[:, :hid], terms[:, hid:]
    factor = 1.0 / jnp.sqrt(jnp.float32(total_rows))
    grad_in = factor * (
        contract_rows(all_tokens, curv_term) + contract_rows(jac_all, gated_hid)
    )
    grad_out = factor * contract_rows(slope_term, sign_all)
    return (grad_in, grad_out)


def solution(mesh):
    fine = Mesh(
        mesh.devices.reshape(16, 2, 2, 2, 4), ("z", "xl", "core", "xh", "y")
    )
    row, col = ("z", "xl", "core"), COL
    return jax.shard_map(
        on_device,
        mesh=fine,
        in_specs=(P(row, col), P(None, col), P(col, row), P(row, col)),
        out_specs=(P(col, row), P(row, col)),
        check_vma=False,
    )
```

```python
import jax
import jax.numpy as jnp
from jax import lax
from jax.sharding import Mesh, PartitionSpec as P

NEAR, COL = ("core", "xl"), ("xh", "y")
BF, F32 = jnp.bfloat16, jnp.float32


def local_terms(hidden, signal):
    cdf_part = 0.5 * (1.0 + lax.erf(hidden * 0.7071067811865476))
    pdf_part = jnp.exp(-0.5 * hidden * hidden) * 0.3989422804014327
    slope_full = cdf_part + hidden * pdf_part
    slopes = slope_full.astype(BF)
    bending = (signal * pdf_part * (2.0 - hidden * hidden)).astype(BF)
    gated = (signal * slope_full).astype(BF)
    return (slopes, bending, gated)


def contract_rows(left, right):
    return lax.dot_general(
        left, right, (((0,), (0,)), ((), ())), preferred_element_type=F32
    )


def contract_cols(left, right):
    return lax.dot_general(
        left, right, (((1,), (1,)), ((), ())), preferred_element_type=F32
    )


def exchange(blocks, axes):
    return lax.all_to_all(blocks, axes, 0, 0, tiled=True)


def gather(block, axes, count):
    rows, cols = block.shape
    return exchange(
        jnp.broadcast_to(block[None], (count, rows, cols)), axes
    ).reshape(count * rows, cols)


def split(array, count):
    rows, cols = array.shape
    return array.astype(BF).reshape(count, rows // count, cols)


def add_up(blocks):
    return blocks.astype(F32).sum(axis=0)


def pair_up(array, name, axis):
    far = lax.ppermute(array, name, [(0, 1), (1, 0)])
    return jnp.where(
        lax.axis_index(name) == 0,
        jnp.concatenate([array, far], axis=axis),
        jnp.concatenate([far, array], axis=axis),
    )


def hand_over(array, name, axis):
    half = array.shape[-1] // 2
    left, right = array[..., :half], array[..., half:]
    first = lax.axis_index(name) == 0
    kept = jnp.where(first, left, right)
    far = lax.ppermute(
        jnp.where(first, right, left), name, [(0, 1), (1, 0)]
    )
    return jnp.where(
        first,
        jnp.concatenate([kept, far], axis=axis),
        jnp.concatenate([far, kept], axis=axis),
    )


def tie(*arrays):
    return lax.optimization_barrier(arrays)


def on_device(tokens, probe_draw, w_in, w_out):
    total_rows = probe_draw.shape[0]
    own_rows, feats = tokens.shape
    nz, nn, nc = (lax.axis_size(a) for a in ("z", NEAR, COL))
    hid = w_in.shape[1]
    wide = nn * hid
    w_in_all = pair_up(pair_up(w_in, "xl", 1), "core", 1)
    w_out_all = pair_up(pair_up(w_out, "xl", 0), "core", 0)
    draw = probe_draw.reshape(nz, nn, own_rows, feats)
    mine = lax.axis_index(("xl", "core"))
    own_draw = lax.dynamic_index_in_dim(draw, mine, axis=1, keepdims=False)
    own_sign = (2 * own_draw - 1).astype(BF).reshape(nz * own_rows, feats)
    signal_part = contract_cols(own_sign, w_out_all)
    own_tokens = gather(tokens, "z", nz)
    hidden_part = jnp.dot(own_tokens, w_in_all, preferred_element_type=F32)
    blocks = split(jnp.concatenate([hidden_part, signal_part], axis=1), nc)
    blocks, draw = tie(blocks, probe_draw)
    sign_all = (
        (2 * draw - 1)
        .astype(BF)
        .reshape(nz, 2, 2, own_rows, feats)
        .transpose(2, 1, 0, 3, 4)
        .reshape(total_rows, feats)
    )
    both, sign_all, w_in_all = tie(exchange(blocks, COL), sign_all, w_in_all)
    both = add_up(both)
    slopes, bending, gated_own = local_terms(both[:, :wide], both[:, wide:])
    gated = gather(gated_own, COL, nc)
    blocks = split(contract_cols(gated, w_in_all), nz)
    blocks, late_tokens, late_gated = tie(blocks, own_tokens, gated)
    token_pair = pair_up(late_tokens, "xl", 0)
    gated_pair = hand_over(late_gated[None], "core", 0)
    jac_sum, token_pair, gated_pair = tie(
        exchange(blocks, "z"), token_pair, gated_pair
    )
    jac_own = add_up(jac_sum).astype(BF)
    all_tokens = pair_up(token_pair, "core", 0)
    gated_hid = hand_over(gated_pair, "xl", 1).reshape(total_rows, hid)
    jac_rows, all_tokens, gated_hid = tie(
        gather(jac_own, "z", nz), all_tokens, gated_hid
    )
    back_part = jnp.dot(jac_rows, w_in_all, preferred_element_type=F32)
    jac_pair = pair_up(jac_rows, "xl", 0)
    back_proj = add_up(exchange(split(back_part, nc), COL))
    rows = back_proj.shape[0]
    curv_own = (back_proj * bending).astype(BF).reshape(rows, nn, hid)
    slope_own = (back_proj * slopes).astype(BF).reshape(rows, nn, hid)
    terms = jnp.concatenate([curv_own, slope_own], axis=2).transpose(1, 0, 2)
    terms = jnp.broadcast_to(terms[:, None], (nn, nc, rows, 2 * hid))
    jac_all = pair_up(jac_pair, "core", 0)
    terms, jac_all = tie(
        exchange(terms.reshape(nn * nc, rows, 2 * hid), NEAR + COL), jac_all
    )
    terms = terms.reshape(total_rows, 2 * hid)
    curv_term, slope_term = terms[:, :hid], terms[:, hid:]
    factor = 1.0 / jnp.sqrt(jnp.float32(total_rows))
    grad_in = factor * (
        contract_rows(all_tokens, curv_term) + contract_rows(jac_all, gated_hid)
    )
    grad_out = factor * contract_rows(slope_term, sign_all)
    return (grad_in, grad_out)


def solution(mesh):
    fine = Mesh(
        mesh.devices.reshape(16, 2, 2, 2, 4), ("z", "xl", "core", "xh", "y")
    )
    row, col = ("z", "xl", "core"), COL
    return jax.shard_map(
        on_device,
        mesh=fine,
        in_specs=(P(row, col), P(None, col), P(col, row), P(row, col)),
        out_specs=(P(col, row), P(row, col)),
        check_vma=False,
    )
```

```python
import jax
import jax.numpy as jnp
from jax import lax
from jax.experimental import pallas as pl
from jax.experimental.pallas import tpu as pltpu
from jax.sharding import Mesh, PartitionSpec as P

NEAR, COL = ("core", "xl"), ("xh", "y")
BF, F32 = jnp.bfloat16, jnp.float32


def local_terms(hidden, signal):
    cdf_part = 0.5 * (1.0 + lax.erf(hidden * 0.7071067811865476))
    pdf_part = jnp.exp(-0.5 * hidden * hidden) * 0.3989422804014327
    slope_full = cdf_part + hidden * pdf_part
    slopes = slope_full.astype(BF)
    bending = (signal * pdf_part * (2.0 - hidden * hidden)).astype(BF)
    gated = (signal * slope_full).astype(BF)
    return (slopes, bending, gated)


def contract_rows(left, right):
    return lax.dot_general(
        left, right, (((0,), (0,)), ((), ())), preferred_element_type=F32
    )


def contract_cols(left, right):
    return lax.dot_general(
        left, right, (((1,), (1,)), ((), ())), preferred_element_type=F32
    )


def exchange(blocks, axes):
    return lax.all_to_all(blocks, axes, 0, 0, tiled=True)


def gather(block, axes, count):
    rows, cols = block.shape
    return exchange(
        jnp.broadcast_to(block[None], (count, rows, cols)), axes
    ).reshape(count * rows, cols)


def split(array, count):
    rows, cols = array.shape
    return array.astype(BF).reshape(count, rows // count, cols)


def add_up(blocks):
    return blocks.astype(F32).sum(axis=0)


def pair_up(array, name, axis):
    far = lax.ppermute(array, name, [(0, 1), (1, 0)])
    return jnp.where(
        lax.axis_index(name) == 0,
        jnp.concatenate([array, far], axis=axis),
        jnp.concatenate([far, array], axis=axis),
    )


def hand_over(array, name, axis):
    half = array.shape[-1] // 2
    left, right = array[..., :half], array[..., half:]
    first = lax.axis_index(name) == 0
    kept = jnp.where(first, left, right)
    far = lax.ppermute(
        jnp.where(first, right, left), name, [(0, 1), (1, 0)]
    )
    return jnp.where(
        first,
        jnp.concatenate([kept, far], axis=axis),
        jnp.concatenate([far, kept], axis=axis),
    )


def tie(*arrays):
    return lax.optimization_barrier(arrays)


def side_by_side(left, right, steps):
    rows, cols = left.shape
    part = rows // steps

    def kernel(left, right, both):
        both[:, :cols] = left[...]
        both[:, cols:] = right[...]

    half = pl.BlockSpec((part, cols), lambda i: (i, 0))
    return pl.pallas_call(
        kernel,
        grid=(steps,),
        out_shape=jax.ShapeDtypeStruct((rows, 2 * cols), BF),
        in_specs=[half, half],
        out_specs=pl.BlockSpec((part, 2 * cols), lambda i: (i, 0)),
        compiler_params=pltpu.CompilerParams(vmem_limit_bytes=8 * 2**20),
        cost_estimate=pl.CostEstimate(
            flops=0, bytes_accessed=8 * rows * cols, transcendentals=0
        ),
    )(left, right)


def on_device(tokens, probe_draw, w_in, w_out):
    total_rows = probe_draw.shape[0]
    own_rows, feats = tokens.shape
    nz, nn, nc = (lax.axis_size(a) for a in ("z", NEAR, COL))
    hid = w_in.shape[1]
    wide = nn * hid
    w_in_all = pair_up(pair_up(w_in, "xl", 1), "core", 1)
    w_out_all = pair_up(pair_up(w_out, "xl", 0), "core", 0)
    draw = probe_draw.reshape(nz, nn, own_rows, feats)
    mine = lax.axis_index(("xl", "core"))
    own_draw = lax.dynamic_index_in_dim(draw, mine, axis=1, keepdims=False)
    own_sign = (2 * own_draw - 1).astype(BF).reshape(nz * own_rows, feats)
    signal_part = contract_cols(own_sign, w_out_all)
    own_tokens = gather(tokens, "z", nz)
    hidden_part = jnp.dot(own_tokens, w_in_all, preferred_element_type=F32)
    blocks = lax.cond(
        lax.axis_index("core") == 0,
        lambda *parts: side_by_side(*parts, 16),
        lambda *parts: side_by_side(*parts, 1),
        hidden_part.astype(BF),
        signal_part.astype(BF),
    )
    blocks = split(blocks, nc)
    blocks, draw = tie(blocks, probe_draw)
    sign_all = (
        (2 * draw - 1)
        .astype(BF)
        .reshape(nz, 2, 2, own_rows, feats)
        .transpose(2, 1, 0, 3, 4)
        .reshape(total_rows, feats)
    )
    both, sign_all, w_in_all = tie(exchange(blocks, COL), sign_all, w_in_all)
    both = add_up(both)
    slopes, bending, gated_own = local_terms(both[:, :wide], both[:, wide:])
    gated = gather(gated_own, COL, nc)
    blocks = split(contract_cols(gated, w_in_all), nz)
    blocks, late_tokens = tie(blocks, own_tokens)
    token_pair = pair_up(late_tokens, "xl", 0)
    jac_sum, token_pair, late_gated = tie(exchange(blocks, "z"), token_pair, gated)
    jac_own = add_up(jac_sum).astype(BF)
    by_xl = late_gated.reshape(-1, 2, 2, hid).transpose(0, 2, 1, 3)
    gated_pair = hand_over(by_xl.reshape(1, -1, wide), "xl", 0)
    jac_rows, gated_pair, token_pair = tie(
        gather(jac_own, "z", nz), gated_pair, token_pair
    )
    back_part = jnp.dot(jac_rows, w_in_all, preferred_element_type=F32)
    jac_pair = pair_up(jac_rows, "xl", 0)
    back_proj = add_up(exchange(split(back_part, nc), COL))
    rows = back_proj.shape[0]
    curv_own = (back_proj * bending).astype(BF).reshape(rows, nn, hid)
    slope_own = (back_proj * slopes).astype(BF).reshape(rows, nn, hid)
    terms = jnp.concatenate([curv_own, slope_own], axis=2).transpose(1, 0, 2)
    terms = jnp.broadcast_to(terms[:, None], (nn, nc, rows, 2 * hid))
    terms, jac_pair, gated_pair, token_pair = tie(
        terms.reshape(nn * nc, rows, 2 * hid), jac_pair, gated_pair, token_pair
    )
    jac_all = pair_up(jac_pair, "core", 0)
    all_tokens = pair_up(token_pair, "core", 0)
    gated_hid = hand_over(gated_pair[None], "core", 0).reshape(total_rows, hid)
    terms, jac_all, all_tokens, gated_hid = tie(
        exchange(terms, NEAR + COL), jac_all, all_tokens, gated_hid
    )
    terms = terms.reshape(total_rows, 2 * hid)
    curv_term, slope_term = terms[:, :hid], terms[:, hid:]
    factor = 1.0 / jnp.sqrt(jnp.float32(total_rows))
    grad_in = factor * (
        contract_rows(all_tokens, curv_term) + contract_rows(jac_all, gated_hid)
    )
    grad_out = factor * contract_rows(slope_term, sign_all)
    return (grad_in, grad_out)


def solution(mesh):
    fine = Mesh(
        mesh.devices.reshape(16, 2, 2, 2, 4), ("z", "xl", "core", "xh", "y")
    )
    row, col = ("z", "xl", "core"), COL
    return jax.shard_map(
        on_device,
        mesh=fine,
        in_specs=(P(row, col), P(None, col), P(col, row), P(row, col)),
        out_specs=(P(col, row), P(row, col)),
        check_vma=False,
    )
```

```python
import jax
import jax.numpy as jnp
from jax import lax
from jax.experimental import pallas as pl
from jax.experimental.pallas import tpu as pltpu
from jax.sharding import Mesh, PartitionSpec as P

NEAR, COL = ("core", "xl"), ("xh", "y")
BF, F32 = jnp.bfloat16, jnp.float32


def local_terms(hidden, signal):
    cdf_part = 0.5 * (1.0 + lax.erf(hidden * 0.7071067811865476))
    pdf_part = jnp.exp(-0.5 * hidden * hidden) * 0.3989422804014327
    slope_full = cdf_part + hidden * pdf_part
    slopes = slope_full.astype(BF)
    bending = (signal * pdf_part * (2.0 - hidden * hidden)).astype(BF)
    gated = (signal * slope_full).astype(BF)
    return (slopes, bending, gated)


def contract_rows(left, right):
    return lax.dot_general(
        left, right, (((0,), (0,)), ((), ())), preferred_element_type=F32
    )


def contract_cols(left, right):
    return lax.dot_general(
        left, right, (((1,), (1,)), ((), ())), preferred_element_type=F32
    )


def exchange(blocks, axes):
    return lax.all_to_all(blocks, axes, 0, 0, tiled=True)


def gather(block, axes, count):
    rows, cols = block.shape
    return exchange(
        jnp.broadcast_to(block[None], (count, rows, cols)), axes
    ).reshape(count * rows, cols)


def split(array, count):
    rows, cols = array.shape
    return array.astype(BF).reshape(count, rows // count, cols)


def add_up(blocks):
    return blocks.astype(F32).sum(axis=0)


def pair_up(array, name, axis):
    far = lax.ppermute(array, name, [(0, 1), (1, 0)])
    return jnp.where(
        lax.axis_index(name) == 0,
        jnp.concatenate([array, far], axis=axis),
        jnp.concatenate([far, array], axis=axis),
    )


def hand_over(array, name, axis):
    half = array.shape[-1] // 2
    left, right = array[..., :half], array[..., half:]
    first = lax.axis_index(name) == 0
    kept = jnp.where(first, left, right)
    far = lax.ppermute(
        jnp.where(first, right, left), name, [(0, 1), (1, 0)]
    )
    return jnp.where(
        first,
        jnp.concatenate([kept, far], axis=axis),
        jnp.concatenate([far, kept], axis=axis),
    )


def tie(*arrays):
    return lax.optimization_barrier(arrays)


def side_by_side(left, right, steps):
    rows, cols = left.shape
    part = rows // steps

    def kernel(left, right, both):
        both[:, :cols] = left[...]
        both[:, cols:] = right[...]

    half = pl.BlockSpec((part, cols), lambda i: (i, 0))
    return pl.pallas_call(
        kernel,
        grid=(steps,),
        out_shape=jax.ShapeDtypeStruct((rows, 2 * cols), BF),
        in_specs=[half, half],
        out_specs=pl.BlockSpec((part, 2 * cols), lambda i: (i, 0)),
        compiler_params=pltpu.CompilerParams(vmem_limit_bytes=8 * 2**20),
        cost_estimate=pl.CostEstimate(
            flops=0, bytes_accessed=8 * rows * cols, transcendentals=0
        ),
    )(left, right)


def last_products(tokens, jac, terms, gated, signs, factor):
    rows, hid = gated.shape
    feats = tokens.shape[1]

    def kernel(
        tokens, jac, terms, gated, signs, grad_in, grad_out,
        terms_here, gated_here, in_here, out_here, sem,
    ):
        get_gated = pltpu.make_async_copy(gated, gated_here, sem.at[0])
        get_terms = pltpu.make_async_copy(terms, terms_here, sem.at[1])
        get_gated.start()
        get_terms.start()
        get_gated.wait()
        in_here[...] = contract_rows(jac[...], gated_here[...])
        get_terms.wait()
        in_here[...] = factor * (
            in_here[...] + contract_rows(tokens[...], terms_here[:, :hid])
        )
        put_in = pltpu.make_async_copy(in_here, grad_in, sem.at[2])
        put_in.start()
        out_here[...] = factor * contract_rows(terms_here[:, hid:], signs[...])
        put_out = pltpu.make_async_copy(out_here, grad_out, sem.at[3])
        put_out.start()
        put_in.wait()
        put_out.wait()

    whole = pl.BlockSpec(memory_space=pltpu.VMEM)
    anywhere = pl.BlockSpec(memory_space=pl.ANY)
    return pl.pallas_call(
        kernel,
        out_shape=(
            jax.ShapeDtypeStruct((feats, hid), F32),
            jax.ShapeDtypeStruct((hid, feats), F32),
        ),
        in_specs=[whole, whole, anywhere, anywhere, whole],
        out_specs=(anywhere, anywhere),
        scratch_shapes=[
            pltpu.VMEM((rows, 2 * hid), BF),
            pltpu.VMEM((rows, hid), BF),
            pltpu.VMEM((feats, hid), F32),
            pltpu.VMEM((hid, feats), F32),
            pltpu.SemaphoreType.DMA((4,)),
        ],
        compiler_params=pltpu.CompilerParams(vmem_limit_bytes=16 * 2**20),
        cost_estimate=pl.CostEstimate(
            flops=6 * rows * hid * feats,
            bytes_accessed=8 * rows * feats + 4 * rows * hid + 8 * hid * feats,
            transcendentals=0,
        ),
    )(tokens, jac, terms, gated, signs)


def on_device(tokens, probe_draw, w_in, w_out):
    total_rows = probe_draw.shape[0]
    own_rows, feats = tokens.shape
    nz, nn, nc = (lax.axis_size(a) for a in ("z", NEAR, COL))
    hid = w_in.shape[1]
    wide = nn * hid
    w_in_all = pair_up(pair_up(w_in, "xl", 1), "core", 1)
    w_out_all = pair_up(pair_up(w_out, "xl", 0), "core", 0)
    draw = probe_draw.reshape(nz, nn, own_rows, feats)
    mine = lax.axis_index(("xl", "core"))
    own_draw = lax.dynamic_index_in_dim(draw, mine, axis=1, keepdims=False)
    own_sign = (2 * own_draw - 1).astype(BF).reshape(nz * own_rows, feats)
    signal_part = contract_cols(own_sign, w_out_all)
    own_tokens = gather(tokens, "z", nz)
    hidden_part = jnp.dot(own_tokens, w_in_all, preferred_element_type=F32)
    blocks = lax.cond(
        lax.axis_index("core") == 0,
        lambda *parts: side_by_side(*parts, 16),
        lambda *parts: side_by_side(*parts, 1),
        hidden_part.astype(BF),
        signal_part.astype(BF),
    )
    blocks = split(blocks, nc)
    blocks, draw = tie(blocks, probe_draw)
    sign_all = (
        (2 * draw - 1)
        .astype(BF)
        .reshape(nz, 2, 2, own_rows, feats)
        .transpose(2, 1, 0, 3, 4)
        .reshape(total_rows, feats)
    )
    both, sign_all, w_in_all = tie(exchange(blocks, COL), sign_all, w_in_all)
    both = add_up(both)
    slopes, bending, gated_own = local_terms(both[:, :wide], both[:, wide:])
    gated = gather(gated_own, COL, nc)
    blocks = split(contract_cols(gated, w_in_all), nz)
    blocks, late_tokens = tie(blocks, own_tokens)
    token_pair = pair_up(late_tokens, "xl", 0)
    jac_sum, token_pair, late_gated = tie(exchange(blocks, "z"), token_pair, gated)
    jac_own = add_up(jac_sum).astype(BF)
    by_xl = late_gated.reshape(-1, 2, 2, hid).transpose(0, 2, 1, 3)
    gated_pair = hand_over(by_xl.reshape(1, -1, wide), "xl", 0)
    jac_rows, gated_pair, token_pair = tie(
        gather(jac_own, "z", nz), gated_pair, token_pair
    )
    back_part = jnp.dot(jac_rows, w_in_all, preferred_element_type=F32)
    jac_pair = pair_up(jac_rows, "xl", 0)
    back_proj = add_up(exchange(split(back_part, nc), COL))
    rows = back_proj.shape[0]
    curv_own = (back_proj * bending).astype(BF).reshape(rows, nn, hid)
    slope_own = (back_proj * slopes).astype(BF).reshape(rows, nn, hid)
    terms = jnp.concatenate([curv_own, slope_own], axis=2).transpose(1, 0, 2)
    terms = jnp.broadcast_to(terms[:, None], (nn, nc, rows, 2 * hid))
    terms, gated_pair, token_pair = tie(
        terms.reshape(nn * nc, rows, 2 * hid), gated_pair, token_pair
    )
    jac_all = pair_up(jac_pair, "core", 0)
    all_tokens = pair_up(token_pair, "core", 0)
    gated_hid = hand_over(gated_pair[None], "core", 0).reshape(total_rows, hid)
    terms, jac_all, all_tokens, gated_hid = tie(
        exchange(terms, NEAR + COL), jac_all, all_tokens, gated_hid
    )
    terms = terms.reshape(total_rows, 2 * hid)
    return last_products(
        all_tokens, jac_all, terms, gated_hid, sign_all, total_rows**-0.5
    )


def solution(mesh):
    fine = Mesh(
        mesh.devices.reshape(16, 2, 2, 2, 4), ("z", "xl", "core", "xh", "y")
    )
    row, col = ("z", "xl", "core"), COL
    return jax.shard_map(
        on_device,
        mesh=fine,
        in_specs=(P(row, col), P(None, col), P(col, row), P(row, col)),
        out_specs=(P(col, row), P(row, col)),
        check_vma=False,
    )
```

```python
import jax
import jax.numpy as jnp
from jax import lax
from jax.experimental import pallas as pl
from jax.experimental.pallas import tpu as pltpu
from jax.sharding import Mesh, PartitionSpec as P

NEAR, COL = ("core", "xl"), ("xh", "y")
BF, F32 = jnp.bfloat16, jnp.float32


def local_terms(hidden, signal):
    cdf_part = 0.5 * (1.0 + lax.erf(hidden * 0.7071067811865476))
    pdf_part = jnp.exp(-0.5 * hidden * hidden) * 0.3989422804014327
    slope_full = cdf_part + hidden * pdf_part
    slopes = slope_full.astype(BF)
    bending = (signal * pdf_part * (2.0 - hidden * hidden)).astype(BF)
    gated = (signal * slope_full).astype(BF)
    return (slopes, bending, gated)


def contract_rows(left, right):
    return lax.dot_general(
        left, right, (((0,), (0,)), ((), ())), preferred_element_type=F32
    )


def contract_cols(left, right):
    return lax.dot_general(
        left, right, (((1,), (1,)), ((), ())), preferred_element_type=F32
    )


def exchange(blocks, axes):
    return lax.all_to_all(blocks, axes, 0, 0, tiled=True)


def gather(block, axes, count):
    rows, cols = block.shape
    return exchange(
        jnp.broadcast_to(block[None], (count, rows, cols)), axes
    ).reshape(count * rows, cols)


def split(array, count):
    rows, cols = array.shape
    return array.astype(BF).reshape(count, rows // count, cols)


def add_up(blocks):
    return blocks.astype(F32).sum(axis=0)


def pair_up(array, name, axis):
    far = lax.ppermute(array, name, [(0, 1), (1, 0)])
    return jnp.where(
        lax.axis_index(name) == 0,
        jnp.concatenate([array, far], axis=axis),
        jnp.concatenate([far, array], axis=axis),
    )


def hand_over(array, name, axis):
    half = array.shape[-1] // 2
    left, right = array[..., :half], array[..., half:]
    first = lax.axis_index(name) == 0
    kept = jnp.where(first, left, right)
    far = lax.ppermute(
        jnp.where(first, right, left), name, [(0, 1), (1, 0)]
    )
    return jnp.where(
        first,
        jnp.concatenate([kept, far], axis=axis),
        jnp.concatenate([far, kept], axis=axis),
    )


def tie(*arrays):
    return lax.optimization_barrier(arrays)


def side_by_side(left, right, part):
    rows, cols = left.shape

    def kernel(left, right, both, made, sem):
        for at in range(0, rows, part):
            now = pl.ds(at, min(part, rows - at))
            made[now, :cols] = left[now, :]
            made[now, cols:] = right[now, :]
            put = pltpu.make_async_copy(made.at[now], both.at[now], sem)
            put.start()
            put.wait()

    whole = pl.BlockSpec(memory_space=pltpu.VMEM)
    return pl.pallas_call(
        kernel,
        out_shape=jax.ShapeDtypeStruct((rows, 2 * cols), BF),
        in_specs=[whole, whole],
        out_specs=pl.BlockSpec(memory_space=pl.ANY),
        scratch_shapes=[
            pltpu.VMEM((rows, 2 * cols), BF),
            pltpu.SemaphoreType.DMA,
        ],
        compiler_params=pltpu.CompilerParams(vmem_limit_bytes=8 * 2**20),
        cost_estimate=pl.CostEstimate(
            flops=0, bytes_accessed=8 * rows * cols, transcendentals=0
        ),
    )(left, right)


def last_products(tokens, jac, terms, gated, signs, factor):
    rows, hid = gated.shape
    feats = tokens.shape[1]

    def kernel(
        tokens, jac, terms, gated, signs, grad_in, grad_out,
        terms_here, gated_here, in_here, out_here, sem,
    ):
        get_gated = pltpu.make_async_copy(gated, gated_here, sem.at[0])
        get_terms = pltpu.make_async_copy(terms, terms_here, sem.at[1])
        get_gated.start()
        get_terms.start()
        get_gated.wait()
        in_here[...] = contract_rows(jac[...], gated_here[...])
        get_terms.wait()
        in_here[...] = factor * (
            in_here[...] + contract_rows(tokens[...], terms_here[:, :hid])
        )
        put_in = pltpu.make_async_copy(in_here, grad_in, sem.at[2])
        put_in.start()
        out_here[...] = factor * contract_rows(terms_here[:, hid:], signs[...])
        put_out = pltpu.make_async_copy(out_here, grad_out, sem.at[3])
        put_out.start()
        put_in.wait()
        put_out.wait()

    whole = pl.BlockSpec(memory_space=pltpu.VMEM)
    anywhere = pl.BlockSpec(memory_space=pl.ANY)
    return pl.pallas_call(
        kernel,
        out_shape=(
            jax.ShapeDtypeStruct((feats, hid), F32),
            jax.ShapeDtypeStruct((hid, feats), F32),
        ),
        in_specs=[whole, whole, anywhere, anywhere, whole],
        out_specs=(anywhere, anywhere),
        scratch_shapes=[
            pltpu.VMEM((rows, 2 * hid), BF),
            pltpu.VMEM((rows, hid), BF),
            pltpu.VMEM((feats, hid), F32),
            pltpu.VMEM((hid, feats), F32),
            pltpu.SemaphoreType.DMA((4,)),
        ],
        compiler_params=pltpu.CompilerParams(vmem_limit_bytes=16 * 2**20),
        cost_estimate=pl.CostEstimate(
            flops=6 * rows * hid * feats,
            bytes_accessed=8 * rows * feats + 4 * rows * hid + 8 * hid * feats,
            transcendentals=0,
        ),
    )(tokens, jac, terms, gated, signs)


def copies(block, count, steps):
    rows, cols = block.shape
    per = count // steps

    def kernel(block, out):
        for k in range(per):
            out[k] = block[...]

    return pl.pallas_call(
        kernel,
        grid=(steps,),
        out_shape=jax.ShapeDtypeStruct((count, rows, cols), BF),
        in_specs=[pl.BlockSpec((rows, cols), lambda i: (0, 0))],
        out_specs=pl.BlockSpec((per, rows, cols), lambda i: (i, 0, 0)),
        compiler_params=pltpu.CompilerParams(vmem_limit_bytes=4 * 2**20),
        cost_estimate=pl.CostEstimate(
            flops=0, bytes_accessed=2 * (count + 1) * rows * cols, transcendentals=0
        ),
    )(block)


def on_device(tokens, probe_draw, w_in, w_out):
    total_rows = probe_draw.shape[0]
    own_rows, feats = tokens.shape
    nz, nn, nc = (lax.axis_size(a) for a in ("z", NEAR, COL))
    hid = w_in.shape[1]
    wide = nn * hid
    w_in_all = pair_up(pair_up(w_in, "xl", 1), "core", 1)
    w_out_all = pair_up(pair_up(w_out, "xl", 0), "core", 0)
    draw = probe_draw.reshape(nz, nn, own_rows, feats)
    mine = lax.axis_index(("xl", "core"))
    own_draw = lax.dynamic_index_in_dim(draw, mine, axis=1, keepdims=False)
    own_sign = (2 * own_draw - 1).astype(BF).reshape(nz * own_rows, feats)
    signal_part = contract_cols(own_sign, w_out_all)
    spread = lax.cond(
        lax.axis_index("core") == 0,
        lambda block: copies(block, nz, 8),
        lambda block: copies(block, nz, 1),
        tokens,
    )
    own_tokens = exchange(spread, "z").reshape(nz * own_rows, feats)
    hidden_part = jnp.dot(own_tokens, w_in_all, preferred_element_type=F32)
    blocks = lax.cond(
        lax.axis_index("core") == 0,
        lambda *parts: side_by_side(*parts, 48),
        lambda *parts: side_by_side(*parts, 256),
        hidden_part.astype(BF),
        signal_part.astype(BF),
    )
    blocks = split(blocks, nc)
    blocks, draw = tie(blocks, probe_draw)
    sign_all = (
        (2 * draw - 1)
        .astype(BF)
        .reshape(nz, 2, 2, own_rows, feats)
        .transpose(2, 1, 0, 3, 4)
        .reshape(total_rows, feats)
    )
    both, sign_all, w_in_all = tie(exchange(blocks, COL), sign_all, w_in_all)
    both = add_up(both)
    slopes, bending, gated_own = local_terms(both[:, :wide], both[:, wide:])
    gated = gather(gated_own, COL, nc)
    blocks = split(contract_cols(gated, w_in_all), nz)
    blocks, late_tokens = tie(blocks, own_tokens)
    token_pair = pair_up(late_tokens, "xl", 0)
    jac_sum, token_pair, late_gated = tie(exchange(blocks, "z"), token_pair, gated)
    jac_own = add_up(jac_sum).astype(BF)
    by_xl = late_gated.reshape(-1, 2, 2, hid).transpose(0, 2, 1, 3)
    gated_pair = hand_over(by_xl.reshape(1, -1, wide), "xl", 0)
    jac_rows, gated_pair, token_pair = tie(
        gather(jac_own, "z", nz), gated_pair, token_pair
    )
    back_part = jnp.dot(jac_rows, w_in_all, preferred_element_type=F32)
    jac_pair = pair_up(jac_rows, "xl", 0)
    back_proj = add_up(exchange(split(back_part, nc), COL))
    rows = back_proj.shape[0]
    curv_own = (back_proj * bending).astype(BF).reshape(rows, nn, hid)
    slope_own = (back_proj * slopes).astype(BF).reshape(rows, nn, hid)
    terms = jnp.concatenate([curv_own, slope_own], axis=2).transpose(1, 0, 2)
    terms = jnp.broadcast_to(terms[:, None], (nn, nc, rows, 2 * hid))
    terms, gated_pair, token_pair = tie(
        terms.reshape(nn * nc, rows, 2 * hid), gated_pair, token_pair
    )
    jac_all = pair_up(jac_pair, "core", 0)
    all_tokens = pair_up(token_pair, "core", 0)
    gated_hid = hand_over(gated_pair[None], "core", 0).reshape(total_rows, hid)
    terms, jac_all, all_tokens, gated_hid = tie(
        exchange(terms, NEAR + COL), jac_all, all_tokens, gated_hid
    )
    terms = terms.reshape(total_rows, 2 * hid)
    return last_products(
        all_tokens, jac_all, terms, gated_hid, sign_all, total_rows**-0.5
    )


def solution(mesh):
    fine = Mesh(
        mesh.devices.reshape(16, 2, 2, 2, 4), ("z", "xl", "core", "xh", "y")
    )
    row, col = ("z", "xl", "core"), COL
    return jax.shard_map(
        on_device,
        mesh=fine,
        in_specs=(P(row, col), P(None, col), P(col, row), P(row, col)),
        out_specs=(P(col, row), P(row, col)),
        check_vma=False,
    )
```

```python
import jax
import jax.numpy as jnp
from jax import lax
from jax.experimental import pallas as pl
from jax.experimental.pallas import tpu as pltpu
from jax.sharding import Mesh, PartitionSpec as P

NEAR, COL = ("core", "xl"), ("xh", "y")
BF, F32 = jnp.bfloat16, jnp.float32


def local_terms(hidden, signal):
    cdf_part = 0.5 * (1.0 + lax.erf(hidden * 0.7071067811865476))
    pdf_part = jnp.exp(-0.5 * hidden * hidden) * 0.3989422804014327
    slope_full = cdf_part + hidden * pdf_part
    slopes = slope_full.astype(BF)
    bending = (signal * pdf_part * (2.0 - hidden * hidden)).astype(BF)
    gated = (signal * slope_full).astype(BF)
    return (slopes, bending, gated)


def contract_rows(left, right):
    return lax.dot_general(
        left, right, (((0,), (0,)), ((), ())), preferred_element_type=F32
    )


def contract_cols(left, right):
    return lax.dot_general(
        left, right, (((1,), (1,)), ((), ())), preferred_element_type=F32
    )


def exchange(blocks, axes):
    return lax.all_to_all(blocks, axes, 0, 0, tiled=True)


def gather(block, axes, count):
    rows, cols = block.shape
    return exchange(
        jnp.broadcast_to(block[None], (count, rows, cols)), axes
    ).reshape(count * rows, cols)


def split(array, count):
    rows, cols = array.shape
    return array.astype(BF).reshape(count, rows // count, cols)


def add_up(blocks):
    return blocks.astype(F32).sum(axis=0)


def pair_up(array, name, axis):
    far = lax.ppermute(array, name, [(0, 1), (1, 0)])
    return jnp.where(
        lax.axis_index(name) == 0,
        jnp.concatenate([array, far], axis=axis),
        jnp.concatenate([far, array], axis=axis),
    )


def hand_over(array, name, axis):
    half = array.shape[-1] // 2
    left, right = array[..., :half], array[..., half:]
    first = lax.axis_index(name) == 0
    kept = jnp.where(first, left, right)
    far = lax.ppermute(
        jnp.where(first, right, left), name, [(0, 1), (1, 0)]
    )
    return jnp.where(
        first,
        jnp.concatenate([kept, far], axis=axis),
        jnp.concatenate([far, kept], axis=axis),
    )


def tie(*arrays):
    return lax.optimization_barrier(arrays)


def side_by_side(left, right, part):
    rows, cols = left.shape

    def kernel(left, right, both, made, sem):
        for at in range(0, rows, part):
            now = pl.ds(at, min(part, rows - at))
            made[now, :cols] = left[now, :]
            made[now, cols:] = right[now, :]
            put = pltpu.make_async_copy(made.at[now], both.at[now], sem)
            put.start()
            put.wait()

    whole = pl.BlockSpec(memory_space=pltpu.VMEM)
    return pl.pallas_call(
        kernel,
        out_shape=jax.ShapeDtypeStruct((rows, 2 * cols), BF),
        in_specs=[whole, whole],
        out_specs=pl.BlockSpec(memory_space=pl.ANY),
        scratch_shapes=[
            pltpu.VMEM((rows, 2 * cols), BF),
            pltpu.SemaphoreType.DMA,
        ],
        compiler_params=pltpu.CompilerParams(vmem_limit_bytes=8 * 2**20),
        cost_estimate=pl.CostEstimate(
            flops=0, bytes_accessed=8 * rows * cols, transcendentals=0
        ),
    )(left, right)


def last_products(tokens, jac, terms, gated, signs, factor):
    rows, hid = gated.shape
    feats = tokens.shape[1]

    def kernel(
        tokens, jac, terms, gated, signs, grad_in, grad_out,
        terms_here, gated_here, in_here, out_here, sem,
    ):
        get_gated = pltpu.make_async_copy(gated, gated_here, sem.at[0])
        get_terms = pltpu.make_async_copy(terms, terms_here, sem.at[1])
        get_gated.start()
        get_terms.start()
        get_gated.wait()
        in_here[...] = contract_rows(jac[...], gated_here[...])
        get_terms.wait()
        in_here[...] = factor * (
            in_here[...] + contract_rows(tokens[...], terms_here[:, :hid])
        )
        put_in = pltpu.make_async_copy(in_here, grad_in, sem.at[2])
        put_in.start()
        out_here[...] = factor * contract_rows(terms_here[:, hid:], signs[...])
        put_out = pltpu.make_async_copy(out_here, grad_out, sem.at[3])
        put_out.start()
        put_in.wait()
        put_out.wait()

    whole = pl.BlockSpec(memory_space=pltpu.VMEM)
    anywhere = pl.BlockSpec(memory_space=pl.ANY)
    return pl.pallas_call(
        kernel,
        out_shape=(
            jax.ShapeDtypeStruct((feats, hid), F32),
            jax.ShapeDtypeStruct((hid, feats), F32),
        ),
        in_specs=[whole, whole, anywhere, anywhere, whole],
        out_specs=(anywhere, anywhere),
        scratch_shapes=[
            pltpu.VMEM((rows, 2 * hid), BF),
            pltpu.VMEM((rows, hid), BF),
            pltpu.VMEM((feats, hid), F32),
            pltpu.VMEM((hid, feats), F32),
            pltpu.SemaphoreType.DMA((4,)),
        ],
        compiler_params=pltpu.CompilerParams(vmem_limit_bytes=16 * 2**20),
        cost_estimate=pl.CostEstimate(
            flops=6 * rows * hid * feats,
            bytes_accessed=8 * rows * feats + 4 * rows * hid + 8 * hid * feats,
            transcendentals=0,
        ),
    )(tokens, jac, terms, gated, signs)


def copies(block, count, steps):
    rows, cols = block.shape
    per = count // steps

    def kernel(block, out):
        for k in range(per):
            out[k] = block[...]

    return pl.pallas_call(
        kernel,
        grid=(steps,),
        out_shape=jax.ShapeDtypeStruct((count, rows, cols), BF),
        in_specs=[pl.BlockSpec((rows, cols), lambda i: (0, 0))],
        out_specs=pl.BlockSpec((per, rows, cols), lambda i: (i, 0, 0)),
        compiler_params=pltpu.CompilerParams(vmem_limit_bytes=4 * 2**20),
        cost_estimate=pl.CostEstimate(
            flops=0, bytes_accessed=2 * (count + 1) * rows * cols, transcendentals=0
        ),
    )(block)


def on_device(tokens, probe_draw, w_in, w_out):
    total_rows = probe_draw.shape[0]
    own_rows, feats = tokens.shape
    nz, nn, nc = (lax.axis_size(a) for a in ("z", NEAR, COL))
    hid = w_in.shape[1]
    wide = nn * hid
    w_in_all = pair_up(pair_up(w_in, "xl", 1), "core", 1)
    w_out_all = pair_up(pair_up(w_out, "xl", 0), "core", 0)
    draw = probe_draw.reshape(nz, nn, own_rows, feats)
    mine = lax.axis_index(("xl", "core"))
    own_draw = lax.dynamic_index_in_dim(draw, mine, axis=1, keepdims=False)
    own_sign = (2 * own_draw - 1).astype(BF).reshape(nz * own_rows, feats)
    signal_part = contract_cols(own_sign, w_out_all)
    spread = lax.cond(
        lax.axis_index("core") == 0,
        lambda block: copies(block, nz, 16),
        lambda block: copies(block, nz, 1),
        tokens,
    )
    own_tokens = exchange(spread, "z").reshape(nz * own_rows, feats)
    hidden_part = jnp.dot(own_tokens, w_in_all, preferred_element_type=F32)
    blocks = lax.cond(
        lax.axis_index("core") == 0,
        lambda *parts: side_by_side(*parts, 64),
        lambda *parts: side_by_side(*parts, 256),
        hidden_part.astype(BF),
        signal_part.astype(BF),
    )
    blocks = split(blocks, nc)
    blocks, draw = tie(blocks, probe_draw)
    sign_all = (
        (2 * draw - 1)
        .astype(BF)
        .reshape(nz, 2, 2, own_rows, feats)
        .transpose(2, 1, 0, 3, 4)
        .reshape(total_rows, feats)
    )
    both, sign_all, w_in_all = tie(exchange(blocks, COL), sign_all, w_in_all)
    both = add_up(both)
    slopes, bending, gated_own = local_terms(both[:, :wide], both[:, wide:])
    gated = gather(gated_own, COL, nc)
    blocks = split(contract_cols(gated, w_in_all), nz)
    blocks, late_tokens = tie(blocks, own_tokens)
    token_pair = pair_up(late_tokens, "xl", 0)
    jac_sum, token_pair, late_gated = tie(exchange(blocks, "z"), token_pair, gated)
    jac_own = add_up(jac_sum).astype(BF)
    by_xl = late_gated.reshape(-1, 2, 2, hid).transpose(0, 2, 1, 3)
    gated_pair = hand_over(by_xl.reshape(1, -1, wide), "xl", 0)
    jac_rows, gated_pair, token_pair = tie(
        gather(jac_own, "z", nz), gated_pair, token_pair
    )
    back_part = jnp.dot(jac_rows, w_in_all, preferred_element_type=F32)
    jac_pair = pair_up(jac_rows, "xl", 0)
    back_proj = add_up(exchange(split(back_part, nc), COL))
    rows = back_proj.shape[0]
    curv_own = (back_proj * bending).astype(BF).reshape(rows, nn, hid)
    slope_own = (back_proj * slopes).astype(BF).reshape(rows, nn, hid)
    terms = jnp.concatenate([curv_own, slope_own], axis=2).transpose(1, 0, 2)
    terms = jnp.broadcast_to(terms[:, None], (nn, nc, rows, 2 * hid))
    terms, gated_pair, token_pair = tie(
        terms.reshape(nn * nc, rows, 2 * hid), gated_pair, token_pair
    )
    jac_all = pair_up(jac_pair, "core", 0)
    all_tokens = pair_up(token_pair, "core", 0)
    gated_hid = hand_over(gated_pair[None], "core", 0).reshape(total_rows, hid)
    terms, jac_all, all_tokens, gated_hid = tie(
        exchange(terms, NEAR + COL), jac_all, all_tokens, gated_hid
    )
    terms = terms.reshape(total_rows, 2 * hid)
    return last_products(
        all_tokens, jac_all, terms, gated_hid, sign_all, total_rows**-0.5
    )


def solution(mesh):
    fine = Mesh(
        mesh.devices.reshape(16, 2, 2, 2, 4), ("z", "xl", "core", "xh", "y")
    )
    row, col = ("z", "xl", "core"), COL
    return jax.shard_map(
        on_device,
        mesh=fine,
        in_specs=(P(row, col), P(None, col), P(col, row), P(row, col)),
        out_specs=(P(col, row), P(row, col)),
        check_vma=False,
    )
```
